32 devices in a mesh: chain: 8 (over z, y), seg: 4 (over x, core).
Axes of the slice: x: 2, y: 2, z: 4, core: 2. Of those that a mesh axis runs over, the one named last changes fastest.
Arguments:
- band_tiles: bfloat16 [8, 1024, 7, 1024], P('chain', None, None, 'seg'), may hold values from -0.009765625 to 0.009765625
- widths: int32 [8], P('chain'), may hold values from 2 to 6, as said below
- warm_start: float32 [8192, 256], P(('chain', 'seg')), may hold values from -4 to 4
- scores: float32 [8192, 64], P(('chain', 'seg')), may hold values from -6 to 6
- penalty: float32 [256], replicated, may hold values from 0.05 to 0.5
Outputs:
- fitted_effects: float32 [8192, 256], P(('chain', 'seg'))
The draws below stay inside these ranges and needn't reach their ends.
Inputs may be any that keep to these rules, and one draw needn't show every extreme that they name: `widths`: each block uses between 2 and 6 forward tiles; both 2 and 6 occur in every draw.
All inputs are finite; a program needn't handle non-finite values.
Results may differ from the reference program's by a relative error of at most 0.00085.
Values may be sent and summed in bfloat16 or wider, within the bound.
A program may use at most 64 MiB of HBM per device.

```python
import math
import jax
import jax.numpy as jnp
from jax import lax

BLOCK = 1024
BAND = 6
TRAITS = 64
PATH = 4
ITERS = 2
NBLK = 8
COLS = 256


def draw_widths(key, part):
    chosen = jax.random.randint(jax.random.fold_in(key, 11), (NBLK,), 2, BAND + 1)
    ranking = jax.random.permutation(jax.random.fold_in(key, 12), NBLK)
    chosen = chosen.at[ranking[0]].set(BAND)
    chosen = chosen.at[ranking[1]].set(2)
    return chosen.astype(jnp.int32)


def level_of(rng, dims, shards, low, high):
    level = 1.0
    for dim, blocks in shards:
        draws = jax.random.uniform(jax.random.fold_in(jax.random.fold_in(rng, 6), dim), (blocks,), jnp.float32, low / len(shards), high / len(shards))
        level = level * jnp.repeat(jnp.exp(draws), dims[dim] // blocks).reshape((-1,) + (1,) * (len(dims) - 1 - dim))
    return level


def scatter_about(stream_key, extent, spread, reach, split=(), held_as=jnp.bfloat16):
    level = level_of(stream_key, extent, split, -0.22, 0.18) if split else 1.0
    values = jax.random.normal(stream_key, extent, jnp.float32) * spread * level
    return jnp.minimum(jnp.maximum(values, -reach), reach).astype(held_as)


def setup_inputs(seed: int = 0) -> dict:
    splits = jax.random.split(jax.random.key(seed), 6)
    return {
        "band_tiles": scatter_about(splits[0], (NBLK, BLOCK, BAND + 1, BLOCK), (416 * BLOCK) ** -0.5, 0.009765625, ((0, 8), (3, 4))),
        "widths": draw_widths(jax.random.fold_in(splits[5], 71), 0),
        "warm_start": scatter_about(splits[2], (NBLK * BLOCK, COLS), 0.5, 4.0, ((0, 32),), jnp.float32),
        "scores": scatter_about(splits[3], (NBLK * BLOCK, TRAITS), 1.0, 6.0, ((0, 32),), jnp.float32),
        "penalty": jnp.clip(jnp.exp(jax.random.uniform(splits[4], (COLS,), jnp.float32, math.log(0.05), math.log(0.5))), 0.05, 0.5),
    }


step_size = 0.8


def soft_limit(values, limit):
    return jnp.sign(values) * jnp.maximum(jnp.abs(values) - limit, 0.0)


def apply_band(band_tiles, widths, estimate):
    columns = estimate.shape[1]
    blocks = estimate.astype(jnp.bfloat16).reshape(NBLK, BLOCK, columns)
    zero_pad = jnp.zeros((BAND, BLOCK, columns), jnp.bfloat16)
    padded = jnp.concatenate([zero_pad, blocks, zero_pad], axis=0)
    offsets = jnp.arange(BAND + 1, dtype=jnp.int32)
    widths = widths.astype(jnp.int32)

    def one_block(block_index):
        tile_block = band_tiles[block_index].astype(jnp.float32)
        forward_blocks = lax.dynamic_slice_in_dim(padded, (block_index + BAND).astype(jnp.int32), BAND + 1, 0).astype(jnp.float32)
        live_mask = (offsets <= widths[block_index]).astype(jnp.float32)
        forward = jnp.einsum("ijk,jkc,j->ic", tile_block, forward_blocks, live_mask, precision=lax.Precision.HIGHEST)
        backward = jnp.zeros((BLOCK, columns), jnp.float32)
        for shift_by in range(BAND + 1):
            source = (block_index - shift_by).astype(jnp.int32)
            clamped = jnp.maximum(source, 0).astype(jnp.int32)
            source_tile = band_tiles[clamped][:, shift_by, :].astype(jnp.float32)
            weight = jnp.where((source >= 0) & (shift_by <= widths[clamped]), 1.0, 0.0).astype(jnp.float32)
            vector = lax.dynamic_index_in_dim(padded, (source + BAND).astype(jnp.int32), 0, keepdims=False).astype(jnp.float32)
            backward = backward + weight * jnp.dot(source_tile.T, vector, precision=lax.Precision.HIGHEST)
        return forward + backward

    result = lax.map(one_block, jnp.arange(NBLK, dtype=jnp.int32))
    return result.reshape(NBLK * BLOCK, columns)


def reference(band_tiles, widths, warm_start, scores, penalty):
    target = jnp.tile(scores, (1, PATH))
    fitted_effects = warm_start
    for iteration in range(ITERS):
        coupled = apply_band(band_tiles, widths, fitted_effects)
        stepped = fitted_effects - step_size * (fitted_effects + coupled - target)
        fitted_effects = soft_limit(stepped, step_size * penalty)
    return fitted_effects
```

```python
import functools

import jax
import jax.numpy as jnp
from jax import lax
from jax.experimental import pallas as pl
from jax.experimental.pallas import tpu as pltpu
from jax.sharding import PartitionSpec as P

ITERS = 2
step_size = 0.8
F32 = jnp.float32
BF16 = jnp.bfloat16


def kernel(
    nchain, nseg, depth,
    tiles_hbm, widths, warm, scores_t, penalty, out,
    tiles, est, target, cur, cur_t, ag, even, odd, acc, rs_send, rs_recv,
    b_send, b_recv, y_send, y_recv, q_send, q_recv,
    tile_sem, ag_s, ag_r, ev_s, ev_r, od_s, od_r, ev_y, rs_s, rs_r, b_s, b_r, y_s, y_r, q_s, q_r,
):
    far = (depth - 1) // 2
    pairs = nchain // 2
    chain, seg = lax.axis_index("chain"), lax.axis_index("seg")
    p, y = chain // 2, chain % 2
    strip = cur.shape[1]
    partner = {"chain": 2 * p + 1 - y, "seg": seg}
    below = {"chain": chain - 2, "seg": seg}
    above = {"chain": chain + 2, "seg": seg}
    has_below, has_above = p >= 1, p + 1 < pairs

    def peer(o):
        return {"chain": chain, "seg": lax.rem(seg + o, nseg)}

    def loads(j):
        return pltpu.make_async_copy(tiles_hbm.at[j], tiles.at[j], tile_sem.at[j])

    for j in range(depth):
        loads(j).start()

    barrier = pltpu.get_barrier_semaphore()

    def greet(device):
        pl.semaphore_signal(barrier, inc=1, device_id=device, device_id_type=pl.DeviceIdType.MESH)

    for o in range(1, nseg):
        greet(peer(o))
    greet(partner)
    pl.when(has_below)(lambda: greet(below))
    pl.when(has_above)(lambda: greet(above))

    est[...] = warm[...]
    zero = jnp.zeros((strip, cur.shape[2]), BF16)
    for it in range(ITERS):
        for d in range(1, far + 1):
            @pl.when(p + d >= pairs)
            def _():
                even[it, d] = zero
                odd[it, d] = zero
        for d in range(far):
            @pl.when(p == 0)
            def _():
                b_recv[it, d, 0] = zero

            @pl.when((p == 0) | ((y == 0) if d == far - 1 else (p == 0)))
            def _():
                b_recv[it, d, 1] = zero

        @pl.when(y == 0)
        def _():
            q_recv[it] = zero

    limit = step_size * penalty[...]
    width = widths[0]

    def live(j):
        return jnp.where(j <= width, 1.0, 0.0).astype(F32)

    def send(src, dst, s_sem, r_sem, device):
        return pltpu.make_async_remote_copy(
            src_ref=src, dst_ref=dst, send_sem=s_sem, recv_sem=r_sem,
            device_id=device, device_id_type=pl.DeviceIdType.MESH,
        )

    pl.semaphore_wait(barrier, nseg + has_below.astype(jnp.int32) + has_above.astype(jnp.int32))

    def iteration(it, carry):
        def ag_copy(o):
            return send(cur_t.at[it], ag.at[it, o - 1], ag_s.at[it, o - 1], ag_r.at[it, o - 1], peer(o))

        def even_copy(d):
            src = cur.at[it] if d == 0 else even.at[it, d]
            return send(src, even.at[it, d + 1], ev_s.at[it, d], ev_r.at[it, d], below)

        def odd_copy(d):
            return send(odd.at[it, d], odd.at[it, d + 1], od_s.at[it, d], od_r.at[it, d], below)

        def cross_copy(d):
            src = cur.at[it] if d == 0 else even.at[it, d]
            return send(src, odd.at[it, d], ev_y.at[it, 0, d], ev_y.at[it, 1, d], partner)

        def up_copy(d, r):
            return send(
                b_send.at[it, d - 1, r], b_recv.at[it, d - 1, r], b_s.at[it, d - 1, r], b_r.at[it, d - 1, r], above
            )

        def y_copy():
            return send(y_send.at[it], y_recv.at[it], y_s.at[it], y_r.at[it], partner)

        def q_copy():
            return send(q_send.at[it], q_recv.at[it], q_s.at[it], q_r.at[it], partner)

        def rs_copy(o):
            return send(rs_send.at[it, o - 1], rs_recv.at[it, o - 1], rs_s.at[it, o - 1], rs_r.at[it, o - 1], peer(o))

        now = est[...]
        cur[it] = now.astype(BF16)
        pl.when(has_below)(lambda: even_copy(0).start())
        pl.when(y == 1)(lambda: cross_copy(0).start())
        cur_t[it] = now.T.astype(BF16)
        for o in range(1, nseg):
            ag_copy(o).start()

        @pl.when(it == 0)
        def _():
            path = cur.shape[2] // scores_t.shape[0]
            target[...] = jnp.concatenate([scores_t[...]] * path, axis=0).T
            for j in range(depth):
                loads(j).wait()

        @pl.when(has_above)
        def _():
            even_copy(0).wait_recv()
            pl.when(has_below)(lambda: even_copy(1).start())
            cross_copy(1).start()

        for o in range(1, nseg):
            ag_copy(o).wait_recv()

        def product(j):
            total = jnp.dot(
                cur_t[it], tiles[j, pl.ds(pl.multiple_of(seg * strip, strip), strip), :], preferred_element_type=F32
            )
            for o in range(1, nseg):
                owner = lax.rem(seg - o + nseg, nseg)
                rows = pl.ds(pl.multiple_of(owner * strip, strip), strip)
                total = total + jnp.dot(ag[it, o - 1], tiles[j, rows, :], preferred_element_type=F32)
            return total * live(j)

        @pl.when(p + far < pairs)
        def _():
            b_send[it, far - 1, 0] = product(2 * far).astype(BF16)
            up_copy(far, 0).start()

            @pl.when(y == 1)
            def _():
                b_send[it, far - 1, 1] = product(2 * far - 1).astype(BF16)
                up_copy(far, 1).start()

        @pl.when(has_above)
        def _():
            cross_copy(1).wait_recv()
            pl.when(has_below)(lambda: odd_copy(1).start())

        def relay_even(d):
            @pl.when(p + d < pairs)
            def _():
                even_copy(d - 1).wait_recv()
                if d < far:
                    pl.when(has_below)(lambda: even_copy(d).start())

        def relay_odd(d):
            def go():
                odd_copy(d - 1).wait_recv()
                if d < far:
                    pl.when(has_below & ((y == 1) | (d + 1 < far)))(lambda: odd_copy(d).start())

            pl.when((p + d < pairs) & ((y == 1) | (d < far)))(go)

        @pl.when(y == 0)
        def _():
            q_send[it] = product(1).astype(BF16)
            q_copy().start()

        for d in range(far - 1, 1, -1):
            relay_even(far + 1 - d)

            @pl.when(p + d < pairs)
            def _():
                value = product(2 * d)
                pl.when(has_below)(lambda: up_copy(d + 1, 0).wait_recv())
                b_send[it, d - 1, 0] = (value + b_recv[it, d, 0].astype(F32)).astype(BF16)
                up_copy(d, 0).start()
                value = product(2 * d + 1 - 2 * y)
                pl.when(has_below & ((y == 1) | (d + 1 < far)))(lambda: up_copy(d + 1, 1).wait_recv())
                b_send[it, d - 1, 1] = (value + b_recv[it, d, 1].astype(F32)).astype(BF16)
                up_copy(d, 1).start()

            relay_odd(far + 1 - d)

        @pl.when(has_above)
        def _():
            value = product(3 - 2 * y)
            pl.when(has_below)(lambda: up_copy(2, 1).wait_recv())
            y_send[it] = (value + b_recv[it, 1, 1].astype(F32)).astype(BF16)
            y_copy().start()

        pl.when(y == 0)(lambda: cross_copy(0).wait_recv())

        def term(rows, j):
            if j == 0:
                held = cur[it]
            elif j % 2 == 0:
                held = even[it, j // 2]
            else:
                held = odd[it, j // 2 + y]
            return jnp.dot(tiles[j, rows, :], held * live(j).astype(BF16), preferred_element_type=F32)

        for q in range(nseg):
            rows = pl.ds(q * strip, strip)
            total = term(rows, 0)
            for j in range(1, 2 * far - 1):
                total = total + term(rows, j)
            acc[rows, :] = total

        @pl.when(has_above)
        def _():
            value = product(2)
            pl.when(has_below)(lambda: up_copy(2, 0).wait_recv())
            y_copy().wait_recv()
            value = value + b_recv[it, 1, 0].astype(F32) + y_recv[it].astype(F32)
            b_send[it, 0, 0] = value.astype(BF16)
            up_copy(1, 0).start()

        relay_even(far)
        relay_odd(far)

        def rest(q):
            rows = pl.ds(pl.multiple_of(q * strip, strip), strip)
            total = acc[rows, :]
            for j in range(2 * far - 1, depth):
                total = total + term(rows, j)
            return total

        for o in range(1, nseg):
            rs_send[it, o - 1] = rest(lax.rem(seg + o, nseg)).astype(BF16)
            rs_copy(o).start()
        forward = rest(seg)
        back = product(0)
        pl.when(has_below)(lambda: up_copy(1, 0).wait_recv())
        pl.when(y == 1)(lambda: q_copy().wait_recv())
        back = back + b_recv[it, 0, 0].astype(F32) + q_recv[it].astype(F32)
        coupled = forward + back.T
        for o in range(1, nseg):
            rs_copy(o).wait_recv()
            coupled = coupled + rs_recv[it, o - 1].astype(F32)
        now = est[...]
        stepped = now - step_size * (now + coupled - target[...])
        est[...] = jnp.where(
            stepped > limit, stepped - limit, jnp.where(stepped < -limit, stepped + limit, 0.0)
        )

        for o in range(1, nseg):
            ag_copy(o).wait_send()
            rs_copy(o).wait_send()

        @pl.when(has_below)
        def _():
            even_copy(0).wait_send()
            for d in range(1, far):
                pl.when(p + d < pairs)(lambda: even_copy(d).wait_send())
                pl.when((p + d < pairs) & ((y == 1) | (d + 1 < far)))(lambda: odd_copy(d).wait_send())

        pl.when(y == 1)(lambda: cross_copy(0).wait_send())
        pl.when(y == 0)(lambda: q_copy().wait_send())

        @pl.when(has_above)
        def _():
            cross_copy(1).wait_send()
            y_copy().wait_send()
            up_copy(1, 0).wait_send()

        for d in range(2, far + 1):
            pl.when(p + d < pairs)(lambda: up_copy(d, 0).wait_send())
            pl.when((p + d < pairs) & ((y == 1) | (d < far)))(lambda: up_copy(d, 1).wait_send())
        return carry

    lax.fori_loop(0, ITERS, iteration, 0)
    out[...] = est[...]


def per_device(nchain, nseg, band_tiles, widths, warm_start, scores, penalty):
    tiles = jnp.transpose(band_tiles[0], (1, 0, 2))
    depth, block, strip = tiles.shape
    far = (depth - 1) // 2
    columns = warm_start.shape[1]
    one = (strip, columns)
    vmem = pl.BlockSpec(memory_space=pltpu.VMEM)
    dma = pltpu.SemaphoreType.DMA
    n = ITERS

    def buf(*lead, dtype=BF16):
        return pltpu.VMEM(lead + one, dtype)

    return pl.pallas_call(
        functools.partial(kernel, nchain, nseg, depth),
        out_shape=jax.ShapeDtypeStruct(one, F32),
        in_specs=[
            pl.BlockSpec(memory_space=pl.ANY), pl.BlockSpec(memory_space=pltpu.SMEM), vmem, vmem, vmem,
        ],
        out_specs=vmem,
        scratch_shapes=[
            pltpu.VMEM((depth, block, strip), BF16),
            buf(dtype=F32), buf(dtype=F32),
            buf(n), pltpu.VMEM((n, columns, strip), BF16), pltpu.VMEM((n, nseg - 1, columns, strip), BF16),
            buf(n, far + 1), buf(n, far + 1),
            pltpu.VMEM((block, columns), F32),
            buf(n, nseg - 1), buf(n, nseg - 1),
            buf(n, far, 2), buf(n, far, 2), buf(n), buf(n), buf(n), buf(n),
            dma((depth,)),
            dma((n, nseg)), dma((n, nseg)),
            dma((n, far)), dma((n, far)), dma((n, far)), dma((n, far)), dma((n, 2, 2)),
            dma((n, nseg)), dma((n, nseg)),
            dma((n, far, 2)), dma((n, far, 2)),
            dma((n,)), dma((n,)), dma((n,)), dma((n,)),
        ],
        compiler_params=pltpu.CompilerParams(
            collective_id=0, has_side_effects=True, vmem_limit_bytes=40 * 1024 * 1024
        ),
    )(tiles, widths, warm_start, scores.T, penalty[None, :])


def solution(mesh):
    in_specs = (
        P("chain", None, None, "seg"),
        P("chain"),
        P(("chain", "seg"), None),
        P(("chain", "seg"), None),
        P(),
    )
    out_specs = P(("chain", "seg"), None)
    return jax.shard_map(
        functools.partial(per_device, mesh.shape["chain"], mesh.shape["seg"]),
        mesh=mesh, in_specs=in_specs, out_specs=out_specs, check_vma=False,
    )
```

```python
import functools

import jax
import jax.numpy as jnp
from jax import lax
from jax.experimental import pallas as pl
from jax.experimental.pallas import tpu as pltpu
from jax.sharding import PartitionSpec as P

ITERS = 2
GROUPS = 2
step_size = 0.8
F32 = jnp.float32
BF16 = jnp.bfloat16


def kernel(
    nchain, nseg, depth,
    tiles_hbm, widths, warm, scores_hbm, penalty_hbm, out,
    tiles, est, scores_t, penalty, target, cur, cur_t, ag, even, odd, acc, rs_send, rs_recv,
    b_send, b_recv, y_send, y_recv, q_send, q_recv,
    tile_sem, in_sem, ag_s, ag_r, ev_s, ev_r, od_s, od_r, ev_y, rs_s, rs_r, b_s, b_r, y_s, y_r, q_s, q_r,
):
    far = (depth - 1) // 2
    pairs = nchain // 2
    chain, seg = lax.axis_index("chain"), lax.axis_index("seg")
    p, y = chain // 2, chain % 2
    strip = cur.shape[1]
    partner = {"chain": 2 * p + 1 - y, "seg": seg}
    below = {"chain": chain - 2, "seg": seg}
    above = {"chain": chain + 2, "seg": seg}
    has_below, has_above = p >= 1, p + 1 < pairs

    def peer(o):
        return {"chain": chain, "seg": lax.rem(seg + o, nseg)}

    def loads(j):
        return pltpu.make_async_copy(tiles_hbm.at[j], tiles.at[j], tile_sem.at[j])

    inputs = [
        pltpu.make_async_copy(src, dst, in_sem.at[i])
        for i, (src, dst) in enumerate(((warm, est), (penalty_hbm, penalty), (scores_hbm, scores_t)))
    ]
    for load in inputs:
        load.start()
    for j in range(depth):
        loads(j).start()

    barrier = pltpu.get_barrier_semaphore()

    def greet(device):
        pl.semaphore_signal(barrier, inc=1, device_id=device, device_id_type=pl.DeviceIdType.MESH)

    for o in range(1, nseg):
        greet(peer(o))
    greet(partner)
    pl.when(has_below)(lambda: greet(below))
    pl.when(has_above)(lambda: greet(above))

    wide = cur.shape[2]
    zero = jnp.zeros((strip, wide), BF16)
    zero_t = jnp.zeros((wide, strip), BF16)
    for it in range(ITERS * GROUPS):
        for d in range(1, far + 1):
            @pl.when(p + d >= pairs)
            def _():
                even[it, d] = zero
                odd[it, d] = zero
        for d in range(far):
            @pl.when(p == 0)
            def _():
                b_recv[it, d, 0] = zero_t

            @pl.when((p == 0) | ((y == 0) if d == far - 1 else (p == 0)))
            def _():
                b_recv[it, d, 1] = zero_t

        @pl.when(y == 0)
        def _():
            q_recv[it] = zero_t

    width = widths[0]

    def live(j):
        return jnp.where(j <= width, 1.0, 0.0).astype(F32)

    def send(src, dst, s_sem, r_sem, device):
        return pltpu.make_async_remote_copy(
            src_ref=src, dst_ref=dst, send_sem=s_sem, recv_sem=r_sem,
            device_id=device, device_id_type=pl.DeviceIdType.MESH,
        )

    pl.semaphore_wait(barrier, nseg + has_below.astype(jnp.int32) + has_above.astype(jnp.int32))

    def transfers(it):
        def ag_copy(o):
            return send(cur_t.at[it], ag.at[it, o - 1], ag_s.at[it, o - 1], ag_r.at[it, o - 1], peer(o))

        def even_copy(d):
            src = cur.at[it] if d == 0 else even.at[it, d]
            return send(src, even.at[it, d + 1], ev_s.at[it, d], ev_r.at[it, d], below)

        def odd_copy(d):
            return send(odd.at[it, d], odd.at[it, d + 1], od_s.at[it, d], od_r.at[it, d], below)

        def cross_copy(d):
            src = cur.at[it] if d == 0 else even.at[it, d]
            return send(src, odd.at[it, d], ev_y.at[it, 0, d], ev_y.at[it, 1, d], partner)

        def up_copy(d, r):
            return send(
                b_send.at[it, d - 1, r], b_recv.at[it, d - 1, r], b_s.at[it, d - 1, r], b_r.at[it, d - 1, r], above
            )

        def y_copy():
            return send(y_send.at[it], y_recv.at[it], y_s.at[it], y_r.at[it], partner)

        def q_copy():
            return send(q_send.at[it], q_recv.at[it], q_s.at[it], q_r.at[it], partner)

        def rs_copy(o):
            return send(rs_send.at[it, o - 1], rs_recv.at[it, o - 1], rs_s.at[it, o - 1], rs_r.at[it, o - 1], peer(o))

        return ag_copy, even_copy, odd_copy, cross_copy, up_copy, y_copy, q_copy, rs_copy

    def iteration(it, columns, first, whole):
        ag_copy, even_copy, odd_copy, cross_copy, up_copy, y_copy, q_copy, rs_copy = transfers(it)
        now = est[:, columns]
        cur[it] = now.astype(BF16)
        pl.when(has_below)(lambda: even_copy(0).start())
        pl.when(y == 1)(lambda: cross_copy(0).start())
        cur_t[it] = now.T.astype(BF16)
        for o in range(1, nseg):
            ag_copy(o).start()

        yield
        if first:
            inputs[1].wait()
            inputs[2].wait()
            path = whole // scores_t.shape[0]
            target[...] = jnp.concatenate([scores_t[...]] * path, axis=0).T
            for j in range(depth):
                loads(j).wait()

        @pl.when(has_above)
        def _():
            even_copy(0).wait_recv()
            pl.when(has_below)(lambda: even_copy(1).start())
            cross_copy(1).start()

        for o in range(1, nseg):
            ag_copy(o).wait_recv()

        def product(j):
            total = jnp.dot(
                cur_t[it], tiles[j, pl.ds(pl.multiple_of(seg * strip, strip), strip), :], preferred_element_type=F32
            )
            for o in range(1, nseg):
                owner = lax.rem(seg - o + nseg, nseg)
                rows = pl.ds(pl.multiple_of(owner * strip, strip), strip)
                total = total + jnp.dot(ag[it, o - 1], tiles[j, rows, :], preferred_element_type=F32)
            return total * live(j)

        @pl.when(p + far < pairs)
        def _():
            b_send[it, far - 1, 0] = product(2 * far).astype(BF16)
            up_copy(far, 0).start()

            @pl.when(y == 1)
            def _():
                b_send[it, far - 1, 1] = product(2 * far - 1).astype(BF16)
                up_copy(far, 1).start()

        yield

        @pl.when(has_above)
        def _():
            cross_copy(1).wait_recv()
            pl.when(has_below)(lambda: odd_copy(1).start())

        def relay_even(d):
            @pl.when(p + d < pairs)
            def _():
                even_copy(d - 1).wait_recv()
                if d < far:
                    pl.when(has_below)(lambda: even_copy(d).start())

        def relay_odd(d):
            def go():
                odd_copy(d - 1).wait_recv()
                if d < far:
                    pl.when(has_below & ((y == 1) | (d + 1 < far)))(lambda: odd_copy(d).start())

            pl.when((p + d < pairs) & ((y == 1) | (d < far)))(go)

        @pl.when(y == 0)
        def _():
            q_send[it] = product(1).astype(BF16)
            q_copy().start()

        for d in range(far - 1, 1, -1):
            yield
            relay_even(far + 1 - d)

            @pl.when(p + d < pairs)
            def _():
                value = product(2 * d)
                pl.when(has_below)(lambda: up_copy(d + 1, 0).wait_recv())
                b_send[it, d - 1, 0] = (value + b_recv[it, d, 0].astype(F32)).astype(BF16)
                up_copy(d, 0).start()
                value = product(2 * d + 1 - 2 * y)
                pl.when(has_below & ((y == 1) | (d + 1 < far)))(lambda: up_copy(d + 1, 1).wait_recv())
                b_send[it, d - 1, 1] = (value + b_recv[it, d, 1].astype(F32)).astype(BF16)
                up_copy(d, 1).start()

            relay_odd(far + 1 - d)

        yield

        @pl.when(has_above)
        def _():
            value = product(3 - 2 * y)
            pl.when(has_below)(lambda: up_copy(2, 1).wait_recv())
            y_send[it] = (value + b_recv[it, 1, 1].astype(F32)).astype(BF16)
            y_copy().start()

        pl.when(y == 0)(lambda: cross_copy(0).wait_recv())

        def term(rows, j):
            if j == 0:
                held = cur[it]
            elif j % 2 == 0:
                held = even[it, j // 2]
            else:
                held = odd[it, j // 2 + y]
            return jnp.dot(tiles[j, rows, :], held * live(j).astype(BF16), preferred_element_type=F32)

        for q in range(nseg):
            rows = pl.ds(q * strip, strip)
            total = term(rows, 0)
            for j in range(1, 2 * far - 1):
                total = total + term(rows, j)
            acc[rows, columns] = total

        yield

        @pl.when(has_above)
        def _():
            value = product(2)
            pl.when(has_below)(lambda: up_copy(2, 0).wait_recv())
            y_copy().wait_recv()
            value = value + b_recv[it, 1, 0].astype(F32) + y_recv[it].astype(F32)
            b_send[it, 0, 0] = value.astype(BF16)
            up_copy(1, 0).start()

        relay_even(far)
        relay_odd(far)
        yield

        def rest(q):
            rows = pl.ds(pl.multiple_of(q * strip, strip), strip)
            total = acc[rows, columns]
            for j in range(2 * far - 1, depth):
                total = total + term(rows, j)
            return total

        for o in range(1, nseg):
            rs_send[it, o - 1] = rest(lax.rem(seg + o, nseg)).astype(BF16)
            rs_copy(o).start()
        forward = rest(seg)
        yield
        back = product(0)
        pl.when(has_below)(lambda: up_copy(1, 0).wait_recv())
        pl.when(y == 1)(lambda: q_copy().wait_recv())
        back = back + b_recv[it, 0, 0].astype(F32) + q_recv[it].astype(F32)
        coupled = forward + back.T
        for o in range(1, nseg):
            rs_copy(o).wait_recv()
            coupled = coupled + rs_recv[it, o - 1].astype(F32)
        now = est[:, columns]
        limit = step_size * penalty[:, columns]
        stepped = now - step_size * (now + coupled - target[:, columns])
        est[:, columns] = jnp.where(
            stepped > limit, stepped - limit, jnp.where(stepped < -limit, stepped + limit, 0.0)
        )

    inputs[0].wait()

    def group(g):
        for i in range(ITERS):
            yield from iteration(i * GROUPS + g, slice(g * wide, (g + 1) * wide), i + g == 0, GROUPS * wide)

    running = [group(g) for g in range(GROUPS)]
    while running:
        running = [one for one in running if next(one, running) is not running]
    out[...] = est[...]

    def drain(it, carry):
        ag_copy, even_copy, odd_copy, cross_copy, up_copy, y_copy, q_copy, rs_copy = transfers(it)
        for o in range(1, nseg):
            ag_copy(o).wait_send()
            rs_copy(o).wait_send()

        @pl.when(has_below)
        def _():
            even_copy(0).wait_send()
            for d in range(1, far):
                pl.when(p + d < pairs)(lambda: even_copy(d).wait_send())
                pl.when((p + d < pairs) & ((y == 1) | (d + 1 < far)))(lambda: odd_copy(d).wait_send())

        pl.when(y == 1)(lambda: cross_copy(0).wait_send())
        pl.when(y == 0)(lambda: q_copy().wait_send())

        @pl.when(has_above)
        def _():
            cross_copy(1).wait_send()
            y_copy().wait_send()
            up_copy(1, 0).wait_send()

        for d in range(2, far + 1):
            pl.when(p + d < pairs)(lambda: up_copy(d, 0).wait_send())
            pl.when((p + d < pairs) & ((y == 1) | (d < far)))(lambda: up_copy(d, 1).wait_send())
        return carry

    lax.fori_loop(0, ITERS * GROUPS, drain, 0)


def per_device(nchain, nseg, band_tiles, widths, warm_start, scores, penalty):
    tiles = jnp.transpose(band_tiles[0], (1, 0, 2))
    depth, block, strip = tiles.shape
    far = (depth - 1) // 2
    columns = warm_start.shape[1]
    wide = columns // GROUPS
    hbm = pl.BlockSpec(memory_space=pltpu.HBM)
    dma = pltpu.SemaphoreType.DMA
    n = ITERS * GROUPS

    def buf(*lead):
        return pltpu.VMEM(lead + (strip, wide), BF16)

    def turned(*lead):
        return pltpu.VMEM(lead + (wide, strip), BF16)

    return pl.pallas_call(
        functools.partial(kernel, nchain, nseg, depth),
        out_shape=jax.ShapeDtypeStruct((strip, columns), F32),
        in_specs=[
            hbm, pl.BlockSpec(memory_space=pltpu.SMEM), hbm, hbm, hbm,
        ],
        out_specs=pl.BlockSpec(memory_space=pltpu.VMEM),
        scratch_shapes=[
            pltpu.VMEM((depth, block, strip), BF16),
            pltpu.VMEM((strip, columns), F32), pltpu.VMEM(scores.shape[::-1], F32), pltpu.VMEM((1, columns), F32),
            pltpu.VMEM((strip, columns), F32),
            buf(n), turned(n), turned(n, nseg - 1),
            buf(n, far + 1), buf(n, far + 1),
            pltpu.VMEM((block, columns), F32),
            buf(n, nseg - 1), buf(n, nseg - 1),
            turned(n, far, 2), turned(n, far, 2), turned(n), turned(n), turned(n), turned(n),
            dma((depth,)), dma((3,)),
            dma((n, nseg)), dma((n, nseg)),
            dma((n, far)), dma((n, far)), dma((n, far)), dma((n, far)), dma((n, 2, 2)),
            dma((n, nseg)), dma((n, nseg)),
            dma((n, far, 2)), dma((n, far, 2)),
            dma((n,)), dma((n,)), dma((n,)), dma((n,)),
        ],
        compiler_params=pltpu.CompilerParams(
            collective_id=0, has_side_effects=True, vmem_limit_bytes=63 * 1024 * 1024
        ),
    )(tiles, widths, warm_start, scores.T, penalty[None, :])


def solution(mesh):
    in_specs = (
        P("chain", None, None, "seg"),
        P("chain"),
        P(("chain", "seg"), None),
        P(("chain", "seg"), None),
        P(),
    )
    out_specs = P(("chain", "seg"), None)
    return jax.shard_map(
        functools.partial(per_device, mesh.shape["chain"], mesh.shape["seg"]),
        mesh=mesh, in_specs=in_specs, out_specs=out_specs, check_vma=False,
    )
```

```python
import functools

import jax
import jax.numpy as jnp
from jax import lax
from jax.experimental import pallas as pl
from jax.experimental.pallas import tpu as pltpu
from jax.sharding import PartitionSpec as P

ITERS = 2
GROUPS = 2
step_size = 0.8
F32 = jnp.float32
BF16 = jnp.bfloat16


def kernel(
    nchain, nseg, depth,
    tiles_hbm, widths, warm, scores_hbm, penalty_hbm, out,
    tiles, est, scores_t, penalty, target, cur, cur_t, ag, even, odd, acc, rs_send, rs_recv,
    b_send, b_recv, y_send, y_recv, q_send, q_recv,
    tile_sem, in_sem, ag_s, ag_r, ev_s, ev_r, od_s, od_r, ev_y, rs_s, rs_r, b_s, b_r, y_s, y_r, q_s, q_r,
):
    far = (depth - 1) // 2
    pairs = nchain // 2
    chain, seg = lax.axis_index("chain"), lax.axis_index("seg")
    p, y = chain // 2, chain % 2
    strip = cur.shape[1]
    partner = {"chain": 2 * p + 1 - y, "seg": seg}
    below = {"chain": chain - 2, "seg": seg}
    above = {"chain": chain + 2, "seg": seg}
    has_below, has_above = p >= 1, p + 1 < pairs

    def facing(o):
        flip = seg if o < 2 else seg + 2 - 4 * (seg // 2)
        return flip + 1 - 2 * (seg % 2) if o % 2 else flip

    def peer(o):
        return {"chain": chain, "seg": facing(o)}

    def loads(j):
        return pltpu.make_async_copy(tiles_hbm.at[j], tiles.at[j], tile_sem.at[j])

    inputs = [
        pltpu.make_async_copy(src, dst, in_sem.at[i])
        for i, (src, dst) in enumerate(((warm, est), (penalty_hbm, penalty), (scores_hbm, scores_t)))
    ]
    for load in inputs:
        load.start()
    for j in range(depth):
        loads(j).start()

    barrier = pltpu.get_barrier_semaphore()

    def greet(device):
        pl.semaphore_signal(barrier, inc=1, device_id=device, device_id_type=pl.DeviceIdType.MESH)

    for o in range(1, nseg):
        greet(peer(o))
    greet(partner)
    pl.when(has_below)(lambda: greet(below))
    pl.when(has_above)(lambda: greet(above))

    wide = cur.shape[2]
    zero = jnp.zeros((strip, wide), BF16)
    zero_t = jnp.zeros((wide, strip), BF16)
    for it in range(ITERS * GROUPS):
        for d in range(1, far + 1):
            @pl.when(p + d >= pairs)
            def _():
                even[it, d] = zero
                odd[it, d] = zero
        for d in range(far):
            @pl.when(p == 0)
            def _():
                b_recv[it, d, 0] = zero_t

            @pl.when((p == 0) | ((y == 0) if d == far - 1 else (p == 0)))
            def _():
                b_recv[it, d, 1] = zero_t

        @pl.when(y == 0)
        def _():
            q_recv[it] = zero_t

    width = widths[0]

    def live(j):
        return jnp.where(j <= width, 1.0, 0.0).astype(F32)

    def send(src, dst, s_sem, r_sem, device):
        return pltpu.make_async_remote_copy(
            src_ref=src, dst_ref=dst, send_sem=s_sem, recv_sem=r_sem,
            device_id=device, device_id_type=pl.DeviceIdType.MESH,
        )

    pl.semaphore_wait(barrier, nseg + has_below.astype(jnp.int32) + has_above.astype(jnp.int32))

    def transfers(it):
        def ag_copy(o):
            src = ag.at[it, 1] if o == 3 else cur_t.at[it]
            return send(src, ag.at[it, o - 1], ag_s.at[it, o - 1], ag_r.at[it, o - 1], peer(o % 2 or 2))

        def even_copy(d):
            src = cur.at[it] if d == 0 else even.at[it, d]
            return send(src, even.at[it, d + 1], ev_s.at[it, d], ev_r.at[it, d], below)

        def odd_copy(d):
            return send(odd.at[it, d], odd.at[it, d + 1], od_s.at[it, d], od_r.at[it, d], below)

        def cross_copy(d):
            src = cur.at[it] if d == 0 else even.at[it, d]
            return send(src, odd.at[it, d], ev_y.at[it, 0, d], ev_y.at[it, 1, d], partner)

        def up_copy(d, r):
            return send(
                b_send.at[it, d - 1, r], b_recv.at[it, d - 1, r], b_s.at[it, d - 1, r], b_r.at[it, d - 1, r], above
            )

        def y_copy():
            return send(y_send.at[it], y_recv.at[it], y_s.at[it], y_r.at[it], partner)

        def q_copy():
            return send(q_send.at[it], q_recv.at[it], q_s.at[it], q_r.at[it], partner)

        def rs_copy(o):
            return send(rs_send.at[it, o - 1], rs_recv.at[it, o - 1], rs_s.at[it, o - 1], rs_r.at[it, o - 1], peer(o % 2 or 2))

        return ag_copy, even_copy, odd_copy, cross_copy, up_copy, y_copy, q_copy, rs_copy

    def iteration(it, columns, first, whole):
        ag_copy, even_copy, odd_copy, cross_copy, up_copy, y_copy, q_copy, rs_copy = transfers(it)
        now = est[:, columns]
        cur[it] = now.astype(BF16)
        pl.when(has_below)(lambda: even_copy(0).start())
        pl.when(y == 1)(lambda: cross_copy(0).start())
        cur_t[it] = now.T.astype(BF16)
        for o in (2, 1):
            ag_copy(o).start()

        yield
        if first:
            inputs[1].wait()
            inputs[2].wait()
            path = whole // scores_t.shape[0]
            target[...] = jnp.concatenate([scores_t[...]] * path, axis=0).T
            for j in range(depth):
                loads(j).wait()

        @pl.when(has_above)
        def _():
            even_copy(0).wait_recv()
            pl.when(has_below)(lambda: even_copy(1).start())
            cross_copy(1).start()

        ag_copy(2).wait_recv()
        ag_copy(3).start()
        ag_copy(1).wait_recv()
        ag_copy(3).wait_recv()

        def product(j):
            total = jnp.dot(
                cur_t[it], tiles[j, pl.ds(pl.multiple_of(seg * strip, strip), strip), :], preferred_element_type=F32
            )
            for o in range(1, nseg):
                owner = facing(o)
                rows = pl.ds(pl.multiple_of(owner * strip, strip), strip)
                total = total + jnp.dot(ag[it, o - 1], tiles[j, rows, :], preferred_element_type=F32)
            return total * live(j)

        @pl.when(p + far < pairs)
        def _():
            b_send[it, far - 1, 0] = product(2 * far).astype(BF16)
            up_copy(far, 0).start()

            @pl.when(y == 1)
            def _():
                b_send[it, far - 1, 1] = product(2 * far - 1).astype(BF16)
                up_copy(far, 1).start()

        yield

        @pl.when(has_above)
        def _():
            cross_copy(1).wait_recv()
            pl.when(has_below)(lambda: odd_copy(1).start())

        def relay_even(d):
            @pl.when(p + d < pairs)
            def _():
                even_copy(d - 1).wait_recv()
                if d < far:
                    pl.when(has_below)(lambda: even_copy(d).start())

        def relay_odd(d):
            def go():
                odd_copy(d - 1).wait_recv()
                if d < far:
                    pl.when(has_below & ((y == 1) | (d + 1 < far)))(lambda: odd_copy(d).start())

            pl.when((p + d < pairs) & ((y == 1) | (d < far)))(go)

        @pl.when(y == 0)
        def _():
            q_send[it] = product(1).astype(BF16)
            q_copy().start()

        for d in range(far - 1, 1, -1):
            yield
            relay_even(far + 1 - d)

            @pl.when(p + d < pairs)
            def _():
                value = product(2 * d)
                pl.when(has_below)(lambda: up_copy(d + 1, 0).wait_recv())
                b_send[it, d - 1, 0] = (value + b_recv[it, d, 0].astype(F32)).astype(BF16)
                up_copy(d, 0).start()
                value = product(2 * d + 1 - 2 * y)
                pl.when(has_below & ((y == 1) | (d + 1 < far)))(lambda: up_copy(d + 1, 1).wait_recv())
                b_send[it, d - 1, 1] = (value + b_recv[it, d, 1].astype(F32)).astype(BF16)
                up_copy(d, 1).start()

            relay_odd(far + 1 - d)

        yield

        @pl.when(has_above)
        def _():
            value = product(3 - 2 * y)
            pl.when(has_below)(lambda: up_copy(2, 1).wait_recv())
            y_send[it] = (value + b_recv[it, 1, 1].astype(F32)).astype(BF16)
            y_copy().start()

        pl.when(y == 0)(lambda: cross_copy(0).wait_recv())

        def term(rows, j):
            if j == 0:
                held = cur[it]
            elif j % 2 == 0:
                held = even[it, j // 2]
            else:
                held = odd[it, j // 2 + y]
            return jnp.dot(tiles[j, rows, :], held * live(j).astype(BF16), preferred_element_type=F32)

        for q in range(nseg):
            rows = pl.ds(q * strip, strip)
            total = term(rows, 0)
            for j in range(1, 2 * far - 1):
                total = total + term(rows, j)
            acc[rows, columns] = total

        yield

        @pl.when(has_above)
        def _():
            value = product(2)
            pl.when(has_below)(lambda: up_copy(2, 0).wait_recv())
            y_copy().wait_recv()
            value = value + b_recv[it, 1, 0].astype(F32) + y_recv[it].astype(F32)
            b_send[it, 0, 0] = value.astype(BF16)
            up_copy(1, 0).start()

        relay_even(far)
        relay_odd(far)
        yield

        def rest(q):
            rows = pl.ds(pl.multiple_of(q * strip, strip), strip)
            total = acc[rows, columns]
            for j in range(2 * far - 1, depth):
                total = total + term(rows, j)
            return total

        for o in (3, 1):
            rs_send[it, o - 1] = rest(facing(o)).astype(BF16)
            rs_copy(o).start()
        across = rest(facing(2))
        rs_copy(3).wait_recv()
        rs_send[it, 1] = (across + rs_recv[it, 2].astype(F32)).astype(BF16)
        rs_copy(2).start()
        forward = rest(seg)
        yield
        back = product(0)
        pl.when(has_below)(lambda: up_copy(1, 0).wait_recv())
        pl.when(y == 1)(lambda: q_copy().wait_recv())
        back = back + b_recv[it, 0, 0].astype(F32) + q_recv[it].astype(F32)
        coupled = forward + back.T
        for o in (1, 2):
            rs_copy(o).wait_recv()
            coupled = coupled + rs_recv[it, o - 1].astype(F32)
        now = est[:, columns]
        limit = step_size * penalty[:, columns]
        stepped = now - step_size * (now + coupled - target[:, columns])
        est[:, columns] = jnp.where(
            stepped > limit, stepped - limit, jnp.where(stepped < -limit, stepped + limit, 0.0)
        )

    inputs[0].wait()

    def group(g):
        for i in range(ITERS):
            yield from iteration(i * GROUPS + g, slice(g * wide, (g + 1) * wide), i + g == 0, GROUPS * wide)

    running = [group(g) for g in range(GROUPS)]
    while running:
        running = [one for one in running if next(one, running) is not running]
    out[...] = est[...]

    def drain(it, carry):
        ag_copy, even_copy, odd_copy, cross_copy, up_copy, y_copy, q_copy, rs_copy = transfers(it)
        for o in range(1, nseg):
            ag_copy(o).wait_send()
            rs_copy(o).wait_send()

        @pl.when(has_below)
        def _():
            even_copy(0).wait_send()
            for d in range(1, far):
                pl.when(p + d < pairs)(lambda: even_copy(d).wait_send())
                pl.when((p + d < pairs) & ((y == 1) | (d + 1 < far)))(lambda: odd_copy(d).wait_send())

        pl.when(y == 1)(lambda: cross_copy(0).wait_send())
        pl.when(y == 0)(lambda: q_copy().wait_send())

        @pl.when(has_above)
        def _():
            cross_copy(1).wait_send()
            y_copy().wait_send()
            up_copy(1, 0).wait_send()

        for d in range(2, far + 1):
            pl.when(p + d < pairs)(lambda: up_copy(d, 0).wait_send())
            pl.when((p + d < pairs) & ((y == 1) | (d < far)))(lambda: up_copy(d, 1).wait_send())
        return carry

    lax.fori_loop(0, ITERS * GROUPS, drain, 0)


def per_device(nchain, nseg, band_tiles, widths, warm_start, scores, penalty):
    tiles = jnp.transpose(band_tiles[0], (1, 0, 2))
    depth, block, strip = tiles.shape
    far = (depth - 1) // 2
    columns = warm_start.shape[1]
    wide = columns // GROUPS
    hbm = pl.BlockSpec(memory_space=pltpu.HBM)
    dma = pltpu.SemaphoreType.DMA
    n = ITERS * GROUPS

    def buf(*lead):
        return pltpu.VMEM(lead + (strip, wide), BF16)

    def turned(*lead):
        return pltpu.VMEM(lead + (wide, strip), BF16)

    return pl.pallas_call(
        functools.partial(kernel, nchain, nseg, depth),
        out_shape=jax.ShapeDtypeStruct((strip, columns), F32),
        in_specs=[
            hbm, pl.BlockSpec(memory_space=pltpu.SMEM), hbm, hbm, hbm,
        ],
        out_specs=pl.BlockSpec(memory_space=pltpu.VMEM),
        scratch_shapes=[
            pltpu.VMEM((depth, block, strip), BF16),
            pltpu.VMEM((strip, columns), F32), pltpu.VMEM(scores.shape[::-1], F32), pltpu.VMEM((1, columns), F32),
            pltpu.VMEM((strip, columns), F32),
            buf(n), turned(n), turned(n, nseg - 1),
            buf(n, far + 1), buf(n, far + 1),
            pltpu.VMEM((block, columns), F32),
            buf(n, nseg - 1), buf(n, nseg - 1),
            turned(n, far, 2), turned(n, far, 2), turned(n), turned(n), turned(n), turned(n),
            dma((depth,)), dma((3,)),
            dma((n, nseg)), dma((n, nseg)),
            dma((n, far)), dma((n, far)), dma((n, far)), dma((n, far)), dma((n, 2, 2)),
            dma((n, nseg)), dma((n, nseg)),
            dma((n, far, 2)), dma((n, far, 2)),
            dma((n,)), dma((n,)), dma((n,)), dma((n,)),
        ],
        compiler_params=pltpu.CompilerParams(
            collective_id=0, has_side_effects=True, vmem_limit_bytes=63 * 1024 * 1024
        ),
    )(tiles, widths, warm_start, scores.T, penalty[None, :])


def solution(mesh):
    in_specs = (
        P("chain", None, None, "seg"),
        P("chain"),
        P(("chain", "seg"), None),
        P(("chain", "seg"), None),
        P(),
    )
    out_specs = P(("chain", "seg"), None)
    return jax.shard_map(
        functools.partial(per_device, mesh.shape["chain"], mesh.shape["seg"]),
        mesh=mesh, in_specs=in_specs, out_specs=out_specs, check_vma=False,
    )
```
